32 devices in a mesh: grp: 8 (over y, x, core), seq: 4 (over z).
Axes of the slice: x: 2, y: 2, z: 4, core: 2. Of those that a mesh axis runs over, the one named last changes fastest.
Arguments:
- inputs: bfloat16 [8, 2, 1536, 768], P('grp', None, 'seq'), may hold values from -6 to 6
- clip_frames: int32 [8, 2], P('grp'), may hold values from 96 to 384, as said below
- cotangent: bfloat16 [8, 2, 1536, 768], P('grp', None, 'seq'), may hold values from -6 to 6
- w_query: bfloat16 [768, 768], P(('grp', 'seq')), may hold values from -0.3125 to 0.3125
- w_key: bfloat16 [768, 768], P(('grp', 'seq')), may hold values from -0.3125 to 0.3125
- w_value: bfloat16 [768, 768], P(('grp', 'seq')), may hold values from -0.21875 to 0.21875
- w_out: bfloat16 [768, 768], P(('grp', 'seq')), may hold values from -0.875 to 0.875
- w_up: bfloat16 [768, 3072], P(('grp', 'seq')), may hold values from -0.21875 to 0.21875
- w_down: bfloat16 [3072, 768], P(('grp', 'seq')), may hold values from -0.15625 to 0.15625
- b_query: bfloat16 [768], P(('grp', 'seq')), may hold values from -3 to 3
- b_value: bfloat16 [768], P(('grp', 'seq')), may hold values from -1.796875 to 1.796875
- b_out: bfloat16 [768], P(('grp', 'seq')), may hold values from -3 to 3
- b_up: bfloat16 [3072], P(('grp', 'seq')), may hold values from -3 to 3
- b_down: bfloat16 [768], P(('grp', 'seq')), may hold values from -3 to 3
- gain_one: bfloat16 [768], P(('grp', 'seq')), may hold values from 0.5 to 1.5
- shift_one: bfloat16 [768], P(('grp', 'seq')), may hold values from -1.796875 to 1.796875
- gain_two: bfloat16 [768], P(('grp', 'seq')), may hold values from 0.5 to 1.5
- shift_two: bfloat16 [768], P(('grp', 'seq')), may hold values from -1.796875 to 1.796875
Outputs:
- layer_out: bfloat16 [8, 2, 1536, 768], P('grp', None, 'seq')
- grad_inputs: bfloat16 [8, 2, 1536, 768], P('grp', None, 'seq')
- grad_w_query: float32 [768, 768], P(('grp', 'seq'))
- grad_w_key: float32 [768, 768], P(('grp', 'seq'))
- grad_w_value: float32 [768, 768], P(('grp', 'seq'))
- grad_w_out: float32 [768, 768], P(('grp', 'seq'))
- grad_w_up: float32 [768, 3072], P(('grp', 'seq'))
- grad_w_down: float32 [3072, 768], P(('grp', 'seq'))
- grad_b_query: float32 [768], P(('grp', 'seq'))
- grad_b_value: float32 [768], P(('grp', 'seq'))
- grad_b_out: float32 [768], P(('grp', 'seq'))
- grad_b_up: float32 [3072], P(('grp', 'seq'))
- grad_b_down: float32 [768], P(('grp', 'seq'))
- grad_gain_one: float32 [768], P(('grp', 'seq'))
- grad_shift_one: float32 [768], P(('grp', 'seq'))
- grad_gain_two: float32 [768], P(('grp', 'seq'))
- grad_shift_two: float32 [768], P(('grp', 'seq'))
The draws below stay inside these ranges and needn't reach their ends.
Inputs may be any that keep to these rules, and one draw needn't show every extreme that they name: Every slice of clip slot (g, s) holds clip_frames[g, s] live frames at its start; in every draw one slot has exactly 384 and another exactly 96.
All inputs are finite; a program needn't handle non-finite values.
Results may differ from the reference program's by a relative error of at most 0.015.
Values may be sent and summed in bfloat16 or wider, within the bound.
A program may use at most 192 MiB of HBM per device.

```python
import jax
import jax.numpy as jnp
from jax import lax

D = 768
HEADS = 12
HEAD = 64
FF = 3072
SLICE = 384
SLOTS = 2
GROUPS = 8
CLIP = 1536
N_SEQ = 4


def draw_clip_frames(key, part):
    key_one, key_two, key_three = jax.random.split(jax.random.fold_in(key, 17), 3)
    total = GROUPS * SLOTS
    counts = jax.random.randint(key_one, (total,), SLICE // 4, SLICE + 1)
    place_one = jax.random.randint(key_two, (), 0, total)
    place_two = (place_one + 1 + jax.random.randint(key_three, (), 0, total - 1)) % total
    spots = jnp.arange(total, dtype=jnp.int32)
    counts = jnp.where(spots == place_one, SLICE, counts)
    counts = jnp.where(spots == place_two, SLICE // 4, counts)
    return counts.reshape(GROUPS, SLOTS).astype(jnp.int32)


def levels(own_key, extent, cuts, smallest, high):
    def one(position, parts):
        heights = jax.random.uniform(jax.random.fold_in(jax.random.fold_in(own_key, 6), position), (parts,), jnp.float32, smallest / len(cuts), high / len(cuts))
        return jnp.repeat(jnp.exp(heights), extent[position] // parts).reshape((-1,) + (1,) * (len(extent) - position - 1))

    loudness = one(*cuts[0])
    for cut in cuts[1:]:
        loudness = loudness * one(*cut)
    return loudness


def scatter_about(key, extent, width, most, cuts=(), held_as=jnp.bfloat16):
    loudness = levels(key, extent, cuts, -0.22, 0.18) if cuts else 1.0
    values = jax.random.normal(key, extent, jnp.float32) * width * loudness
    return jnp.minimum(jnp.maximum(values, -most), most).astype(held_as)


def setup_inputs(seed: int = 0) -> dict:
    seeds = jax.random.split(jax.random.key(seed), 19)
    return {
        "inputs": scatter_about(seeds[0], (GROUPS, SLOTS, CLIP, D), 1.0, 6.0, ((0, 8), (2, 4))),
        "clip_frames": draw_clip_frames(jax.random.fold_in(seeds[18], 71), 0),
        "cotangent": scatter_about(seeds[2], (GROUPS, SLOTS, CLIP, D), 1.0, 6.0, ((0, 8), (2, 4))),
        "w_query": scatter_about(seeds[3], (D, D), (D // 2) ** -0.5, 0.3125, ((0, 32),)),
        "w_key": scatter_about(seeds[4], (D, D), (D // 2) ** -0.5, 0.3125, ((0, 32),)),
        "w_value": scatter_about(seeds[5], (D, D), D ** -0.5, 0.21875, ((0, 32),)),
        "w_out": scatter_about(seeds[6], (D, D), (D // 16) ** -0.5, 0.875, ((0, 32),)),
        "w_up": scatter_about(seeds[7], (D, FF), D ** -0.5, 0.21875, ((0, 32),)),
        "w_down": scatter_about(seeds[8], (FF, D), (FF // 2) ** -0.5, 0.15625, ((0, 32),)),
        "b_query": scatter_about(seeds[9], (D,), 0.5, 3.0, ((0, 32),)),
        "b_value": scatter_about(seeds[10], (D,), 0.3, 1.796875, ((0, 32),)),
        "b_out": scatter_about(seeds[11], (D,), 0.5, 3.0, ((0, 32),)),
        "b_up": scatter_about(seeds[12], (FF,), 0.5, 3.0, ((0, 32),)),
        "b_down": scatter_about(seeds[13], (D,), 0.5, 3.0, ((0, 32),)),
        "gain_one": jnp.clip(1.0 + 0.1 * jax.random.normal(seeds[14], (D,), jnp.float32), 0.5, 1.5).astype(jnp.bfloat16),
        "shift_one": scatter_about(seeds[15], (D,), 0.3, 1.796875, ((0, 32),)),
        "gain_two": jnp.clip(1.0 + 0.1 * jax.random.normal(seeds[16], (D,), jnp.float32), 0.5, 1.5).astype(jnp.bfloat16),
        "shift_two": scatter_about(seeds[17], (D,), 0.3, 1.796875, ((0, 32),)),
    }


epsilon = 1e-05
score_scale = 0.125

@jax.custom_vjp
def low(v):
    return lax.optimization_barrier(v.astype(jnp.bfloat16)).astype(jnp.float32)

@jax.custom_vjp
def low_back(v):
    return v

def low_keep(v):
    return (low(v), None)

def low_pass(kept, grad):
    return (grad,)

def back_keep(v):
    return (v, None)

def back_low(kept, grad):
    return (low(grad),)
low.defvjp(low_keep, low_pass)
low_back.defvjp(back_keep, back_low)

def round_both(value):
    return low_back(low(value))

def matmul(left, right):
    return jnp.dot(left, right, precision=lax.Precision.HIGHEST, preferred_element_type=jnp.float32)

def norm_rows(token_rows, gain_vec, shift_vec):
    row_mean = lax.optimization_barrier(jnp.mean(token_rows, -1, keepdims=True))
    centred = token_rows - row_mean
    inverse = lax.rsqrt(lax.optimization_barrier(jnp.mean(centred * centred, -1, keepdims=True)) + epsilon)
    return centred * inverse * gain_vec + shift_vec

def one_clip(params, clip_rows, live_keys):
    w_query, w_key, w_value, w_out, w_up, w_down, b_query, b_value, b_out, b_up, b_down, gain_one, shift_one, gain_two, shift_two = params
    length = clip_rows.shape[0]
    first = low(norm_rows(clip_rows, gain_one, shift_one))
    queries = round_both(matmul(first, w_query) + b_query).reshape(length, HEADS, HEAD)
    key_rows = round_both(matmul(first, w_key)).reshape(length, HEADS, HEAD)
    value_rows = round_both(matmul(first, w_value) + b_value).reshape(length, HEADS, HEAD)
    scores = jnp.einsum('qhd,khd->hqk', queries, key_rows, precision=lax.Precision.HIGHEST) * score_scale
    scores = low_back(scores)
    scores = jnp.where(live_keys[None, None, :], scores, -1e+30)
    row_max = lax.optimization_barrier(jnp.max(scores, -1, keepdims=True))
    exponent = jnp.exp(scores - row_max)
    weights = low(exponent / lax.optimization_barrier(jnp.sum(exponent, -1, keepdims=True)))
    mixed = jnp.einsum('hqk,khd->qhd', weights, value_rows, precision=lax.Precision.HIGHEST)
    mixed = round_both(mixed.reshape(length, D))
    branch = low_back(matmul(mixed, w_out) + b_out)
    middle = clip_rows + branch
    second = low(norm_rows(middle, gain_two, shift_two))
    hidden = low_back(matmul(second, w_up) + b_up)
    active = low(jax.nn.gelu(hidden, approximate=False))
    feed = low_back(matmul(active, w_down) + b_down)
    return middle + feed

def reference(inputs, clip_frames, cotangent, w_query, w_key, w_value, w_out, w_up, w_down, b_query, b_value, b_out, b_up, b_down, gain_one, shift_one, gain_two, shift_two):
    params = tuple((weight.astype(jnp.float32) for weight in (w_query, w_key, w_value, w_out, w_up, w_down, b_query, b_value, b_out, b_up, b_down, gain_one, shift_one, gain_two, shift_two)))
    clips = inputs.astype(jnp.float32).reshape(GROUPS * SLOTS, N_SEQ * SLICE, D)
    offsets = jnp.arange(N_SEQ * SLICE, dtype=jnp.int32) % SLICE
    live = offsets[None, :] < clip_frames.reshape(GROUPS * SLOTS, 1)

    def forward(clip_data, weights):

        def clip_step(clip_item):
            return one_clip(weights, clip_item[0], clip_item[1])
        return lax.map(jax.checkpoint(clip_step), (clip_data, live))
    outputs, pullback = jax.vjp(forward, clips, params)
    upstream = cotangent.astype(jnp.float32).reshape(clips.shape)
    grad_clips, grad_params = pullback(upstream)
    full_shape = inputs.shape
    return (outputs.reshape(full_shape).astype(jnp.bfloat16), grad_clips.reshape(full_shape).astype(jnp.bfloat16), grad_params[0], grad_params[1], grad_params[2], grad_params[3], grad_params[4], grad_params[5], grad_params[6], grad_params[7], grad_params[8], grad_params[9], grad_params[10], grad_params[11], grad_params[12], grad_params[13], grad_params[14])
```

```python
import functools

import jax
import jax.numpy as jnp
from jax import lax
from jax.experimental import pallas as pl
from jax.experimental.pallas import tpu as pltpu
from jax.sharding import PartitionSpec as P

HEAD = 64


epsilon = 1e-05
score_scale = 0.125
sqrt_half = 0.7071067811865476
inv_root_tau = 0.3989422804014327


def standardize(token_rows):
    row_mean = jnp.mean(token_rows, -1, keepdims=True)
    centred = token_rows - row_mean
    inverse = lax.rsqrt(jnp.mean(centred * centred, -1, keepdims=True) + epsilon)
    return (centred * inverse, inverse)


def norm_back(grad_out, normed, inverse, gain_vec):
    scaled = grad_out * gain_vec
    grad_rows = inverse * (
        scaled
        - jnp.mean(scaled, -1, keepdims=True)
        - normed * jnp.mean(scaled * normed, -1, keepdims=True)
    )
    return (grad_rows, jnp.sum(grad_out * normed, 0), jnp.sum(grad_out, 0))


def gelu_slope(hidden):
    return (
        0.5 * (1.0 + lax.erf(hidden * sqrt_half))
        + hidden * jnp.exp(-0.5 * hidden * hidden) * inv_root_tau
    )


PAIR = 2 * HEAD
Q_BLOCK = 256
NT = (((1,), (1,)), ((), ()))
f32 = jnp.float32
bf16 = jnp.bfloat16


def head_mask(head, width):
    lane = lax.broadcasted_iota(jnp.int32, (1, width), 1)
    chosen = lane < HEAD if head == 0 else lane >= HEAD
    return chosen.astype(f32).astype(bf16)


def nt(left, right):
    return lax.dot_general(left, right, NT, preferred_element_type=f32)


def attend_kernel(q_ref, ko_ref, kx_ref, vo_ref, vx_ref, bias_ref, out_ref, lse_ref):
    queries = q_ref[...] * jnp.asarray(score_scale, bf16)
    keys = jnp.concatenate([ko_ref[...], kx_ref[...]], 0)
    values_t = jnp.concatenate([vo_ref[...], vx_ref[...]], 0).T
    bias = jnp.concatenate([bias_ref[...]] * 2, 0)
    mixed = []
    for head in range(2):
        scores = nt(keys, queries * head_mask(head, PAIR)) + bias
        row_max = jnp.max(scores, 0, keepdims=True)
        exponent = jnp.exp(scores - row_max)
        row_sum = jnp.sum(exponent, 0, keepdims=True)
        part = jnp.dot(
            values_t[head * HEAD : (head + 1) * HEAD],
            exponent.astype(bf16),
            preferred_element_type=f32,
        )
        mixed.append(part * (1.0 / row_sum))
        lse_ref[0, head : head + 1, :] = row_max + jnp.log(row_sum)
    out_ref[...] = jnp.concatenate(mixed, 0).T.astype(bf16)


def attend_back_kernel(
    q_ref, ko_ref, kx_ref, vo_ref, vx_ref, bias_ref, out_ref, grad_ref, lse_ref,
    dq_ref, dko_ref, dvo_ref, dkx_ref, dvx_ref, dk_acc, dv_acc,
):
    step = pl.program_id(1)
    queries = q_ref[...] * jnp.asarray(score_scale, bf16)
    grads = grad_ref[...]
    keys = jnp.concatenate([ko_ref[...], kx_ref[...]], 0)
    keys_t = keys.T
    values = jnp.concatenate([vo_ref[...], vx_ref[...]], 0)
    bias = jnp.concatenate([bias_ref[...]] * 2, 0)
    inner = (grads.astype(f32) * out_ref[...].astype(f32)).T
    grad_queries = []
    grad_keys = grad_values = None
    for head in range(2):
        mask = head_mask(head, PAIR)
        rows = slice(head * HEAD, (head + 1) * HEAD)
        query_head, grad_head = queries * mask, grads * mask
        scores = nt(keys, query_head) + bias
        weights = jnp.exp(scores - lse_ref[0, head : head + 1, :])
        inner_sum = jnp.sum(inner[rows], 0, keepdims=True)
        grad_scores = (weights * (nt(values, grad_head) - inner_sum)).astype(bf16)
        value_part = jnp.dot(weights.astype(bf16), grad_head, preferred_element_type=f32)
        key_part = jnp.dot(grad_scores, query_head, preferred_element_type=f32)
        grad_values = value_part if head == 0 else grad_values + value_part
        grad_keys = key_part if head == 0 else grad_keys + key_part
        grad_queries.append(jnp.dot(keys_t[rows], grad_scores, preferred_element_type=f32))
    dq_ref[...] = (jnp.concatenate(grad_queries, 0).T * score_scale).astype(bf16)

    @pl.when(step == 0)
    def _():
        dk_acc[...] = grad_keys
        dv_acc[...] = grad_values

    @pl.when(step > 0)
    def _():
        dk_acc[...] += grad_keys
        dv_acc[...] += grad_values

    @pl.when(step == pl.num_programs(1) - 1)
    def _():
        half = dko_ref.shape[0]
        dko_ref[...] = dk_acc[:half].astype(bf16)
        dkx_ref[...] = dk_acc[half:].astype(bf16)
        dvo_ref[...] = dv_acc[:half].astype(bf16)
        dvx_ref[...] = dv_acc[half:].astype(bf16)


def attention_specs(rows, pairs, first):
    whole = lambda shift: pl.BlockSpec((rows, PAIR), lambda p, i: (0, p + first + shift))
    return [
        pl.BlockSpec((Q_BLOCK, PAIR), lambda p, i: (i, p + first)),
        whole(pairs),
        whole(0),
        whole(2 * pairs),
        whole(pairs),
        pl.BlockSpec((rows, Q_BLOCK), lambda p, i: (0, 0)),
    ]


def attend(qkv, kv_other, bias):
    rows, width = qkv.shape[0], qkv.shape[1] // 3
    pairs = width // PAIR
    return pl.pallas_call(
        attend_kernel,
        grid=(pairs, rows // Q_BLOCK),
        in_specs=attention_specs(rows, pairs, 0),
        out_specs=[
            pl.BlockSpec((Q_BLOCK, PAIR), lambda p, i: (i, p)),
            pl.BlockSpec((1, 8, Q_BLOCK), lambda p, i: (p, 0, i)),
        ],
        out_shape=[
            jax.ShapeDtypeStruct((rows, width), bf16),
            jax.ShapeDtypeStruct((pairs, 8, rows), f32),
        ],
        compiler_params=pltpu.CompilerParams(vmem_limit_bytes=40 * 2**20),
        cost_estimate=pl.CostEstimate(
            flops=32 * rows * rows * width,
            bytes_accessed=14 * rows * width,
            transcendentals=2 * rows * rows * width // HEAD,
        ),
    )(qkv, qkv, kv_other, qkv, kv_other, bias)


def attend_back(qkv, kv_other, bias, mixed, grads, lse, first, count):
    rows, width = mixed.shape
    pairs = width // PAIR
    block = lambda: pl.BlockSpec((Q_BLOCK, PAIR), lambda p, i: (i, p + first))
    return pl.pallas_call(
        attend_back_kernel,
        grid=(count, rows // Q_BLOCK),
        in_specs=attention_specs(rows, pairs, first)
        + [block(), block(), pl.BlockSpec((1, 8, Q_BLOCK), lambda p, i: (p + first, 0, i))],
        out_specs=[pl.BlockSpec((Q_BLOCK, PAIR), lambda p, i: (i, p))]
        + [pl.BlockSpec((rows, PAIR), lambda p, i: (0, p))] * 4,
        out_shape=[jax.ShapeDtypeStruct((rows, count * PAIR), bf16)] * 5,
        scratch_shapes=[pltpu.VMEM((2 * rows, PAIR), f32)] * 2,
        compiler_params=pltpu.CompilerParams(vmem_limit_bytes=40 * 2**20),
        cost_estimate=pl.CostEstimate(
            flops=80 * rows * rows * count * PAIR,
            bytes_accessed=24 * rows * count * PAIR,
            transcendentals=4 * rows * rows * count,
        ),
    )(qkv, qkv, kv_other, qkv, kv_other, bias, mixed, grads, lse)


def pick(block, index, axis):
    return lax.dynamic_index_in_dim(block, index, axis, keepdims=False)


def scatter_sum(total, grp_size, seq_size):
    grp, seq = lax.axis_index("grp"), lax.axis_index("seq")
    unit, columns = total.shape[0] // grp_size, total.shape[1]
    left, bit = grp_size, 1
    while left > 1:
        left //= 2
        total = total.reshape(left, 2, unit, columns)
        mine = (grp // bit) % 2
        arrived = lax.ppermute(
            pick(total, 1 - mine, 1).astype(bf16), "grp", [(i, i ^ bit) for i in range(grp_size)]
        )
        total = pick(total, mine, 1) + arrived.astype(f32)
        bit *= 2
    total = total.reshape(seq_size, unit // seq_size, columns)
    result = pick(total, seq, 0)
    for offset in range(1, seq_size):
        arrived = lax.ppermute(
            pick(total, (seq + offset) % seq_size, 0).astype(bf16),
            "seq",
            [(i, (i + offset) % seq_size) for i in range(seq_size)],
        )
        result = result + arrived.astype(f32)
    return result


def body(
    grp_size, seq_size,
    inputs, clip_frames, cotangent,
    w_query, w_key, w_value, w_out, w_up, w_down,
    b_query, b_value, b_out, b_up, b_down,
    gain_one, shift_one, gain_two, shift_two,
):
    axes = ("grp", "seq")
    slot_count, slice_len, width = inputs.shape[1:]
    hidden_width = w_up.shape[1]
    depth = w_query.shape[0]
    spread = hidden_width // width
    row_count = slot_count * slice_len
    grp, seq = lax.axis_index("grp"), lax.axis_index("seq")

    def route(flip):
        moves = []
        for g in range(grp_size):
            for s in range(seq_size):
                slot = (s + flip) % 2
                target = (g // 2 * 2 + s // 2) * seq_size + g % 2 * 2 + slot
                moves.append((g * seq_size + s, target))
        return moves

    routes = (route(0), route(1))
    back_routes = tuple([(b, a) for a, b in moves] for moves in routes)
    swap = [(g, g ^ 1) for g in range(grp_size)]
    parity = seq % 2

    def to_clip(block):
        return jnp.concatenate(
            [
                lax.ppermute(pick(block[0], (parity + flip) % 2, 0), axes, routes[flip])
                for flip in range(2)
            ],
            0,
        )

    def from_clip(rows):
        same, other = (
            lax.ppermute(rows[flip * slice_len : (flip + 1) * slice_len], axes, back_routes[flip])
            for flip in range(2)
        )
        even = parity == 0
        return jnp.stack([jnp.where(even, same, other), jnp.where(even, other, same)])[None]

    vectors = jnp.stack(
        [b_query, b_value, b_out, b_down, gain_one, shift_one, gain_two, shift_two], 1
    )
    vectors = jnp.concatenate([vectors, b_up.reshape(depth, spread)], 1)
    vectors = jnp.pad(vectors, ((0, 0), (0, 128 - vectors.shape[1])))
    early = lax.all_gather(
        jnp.concatenate([w_query, w_key, w_value, vectors], 1), axes, axis=0, tiled=True
    )
    late_shard = jnp.concatenate([w_out, w_up, w_down.reshape(depth, hidden_width)], 1)
    early, late_shard = lax.optimization_barrier((early, late_shard))
    late = lax.all_gather(late_shard, axes, axis=0, tiled=True)
    w_qkv = early[:, : 3 * width]
    columns = early[:, 3 * width :].astype(f32).T
    bq, bv, bo, bd, gain_first, shift_first, gain_second, shift_second = (
        columns[i] for i in range(8)
    )
    bu = columns[8 : 8 + spread].T.reshape(hidden_width)
    wo_full = late[:, :width]
    up_full = late[:, width : width + hidden_width]
    down_full = late[:, width + hidden_width :].reshape(hidden_width, width)

    frames_other = lax.ppermute(clip_frames, "grp", swap)
    frames = jnp.where(seq // 2 == grp % 2, clip_frames, frames_other)[0]
    frame_count = jnp.where(parity == 0, frames[0], frames[1])
    offsets = jnp.arange(row_count, dtype=jnp.int32) % slice_len
    bias = jnp.broadcast_to(
        jnp.where(offsets < frame_count, 0.0, -1e30).astype(f32)[:, None], (row_count, Q_BLOCK)
    )

    token_rows = to_clip(inputs).astype(f32)
    grad_top = to_clip(cotangent)
    normed_one, inverse_one = standardize(token_rows)
    first_in = (normed_one * gain_first + shift_first).astype(bf16)
    b_qkv = jnp.concatenate([bq, jnp.zeros_like(bq), bv])
    qkv = (jnp.dot(first_in, w_qkv, preferred_element_type=f32) + b_qkv).astype(bf16)
    kv_other = lax.ppermute(qkv[:, width:], "grp", swap)
    mixed_low, lse = attend(qkv, kv_other, bias)
    middle = token_rows + jnp.dot(mixed_low, wo_full, preferred_element_type=f32) + bo
    normed_two, inverse_two = standardize(middle)
    second_in = (normed_two * gain_second + shift_second).astype(bf16)
    hidden = jnp.dot(second_in, up_full, preferred_element_type=f32) + bu
    active_low = jax.nn.gelu(hidden, approximate=False).astype(bf16)
    result = middle + jnp.dot(active_low, down_full, preferred_element_type=f32) + bd
    layer_out = from_clip(result.astype(bf16))

    grad_rows = grad_top.astype(f32)
    grad_down = jnp.dot(active_low.T, grad_top, preferred_element_type=f32)
    gbias_down = jnp.sum(grad_rows, 0)
    grad_active = jnp.dot(grad_top, down_full.T, preferred_element_type=f32)
    grad_hidden = (grad_active * gelu_slope(hidden)).astype(bf16)
    grad_up = jnp.dot(second_in.T, grad_hidden, preferred_element_type=f32)
    gbias_up = jnp.sum(grad_hidden.astype(f32), 0)
    grad_second = jnp.dot(grad_hidden, up_full.T, preferred_element_type=f32)
    grad_norm_two, grad_gain_two, grad_shift_two = norm_back(
        grad_second, normed_two, inverse_two, gain_second
    )
    grad_middle = grad_rows + grad_norm_two
    grad_branch = grad_middle.astype(bf16)
    grad_out = jnp.dot(mixed_low.T, grad_branch, preferred_element_type=f32)
    gbias_out = jnp.sum(grad_branch.astype(f32), 0)
    grad_mixed = jnp.dot(grad_branch, wo_full.T, preferred_element_type=f32).astype(bf16)

    out_down = scatter_sum(grad_down, grp_size, seq_size)
    out_up = scatter_sum(grad_up, grp_size, seq_size)
    out_out = scatter_sum(grad_out, grp_size, seq_size)

    pairs = width // PAIR
    count = 1
    grad_q, grad_k, grad_v = [], [], []
    for start in range(0, pairs, count):
        dq, dko, dvo, dkx, dvx = attend_back(
            qkv, kv_other, bias, mixed_low, grad_mixed, lse, start, count
        )
        grad_q.append(dq)
        for own, other, kept in ((dko, dkx, grad_k), (dvo, dvx, grad_v)):
            arrived = lax.ppermute(other, "grp", swap)
            kept.append((own.astype(f32) + arrived.astype(f32)).astype(bf16))
    grad_qkv = jnp.concatenate(grad_q + grad_k + grad_v, 1)
    gw_qkv = jnp.dot(first_in.T, grad_qkv, preferred_element_type=f32)
    gbias_qkv = jnp.sum(grad_qkv.astype(f32), 0)
    grad_first = lax.dot_general(grad_qkv, w_qkv, NT, preferred_element_type=f32)
    grad_norm_one, grad_gain_one, grad_shift_one = norm_back(
        grad_first, normed_one, inverse_one, gain_first
    )
    grad_inputs = from_clip((grad_middle + grad_norm_one).astype(bf16))
    sums = jnp.stack(
        [
            gbias_qkv[:width], gbias_qkv[2 * width :], gbias_out, gbias_down,
            grad_gain_one, grad_shift_one, grad_gain_two, grad_shift_two,
        ]
    )
    sums = jnp.concatenate([sums, gbias_up.reshape(width, spread).T], 0)
    sums = jnp.pad(sums, ((0, 128 - sums.shape[0]), (0, 0))).T
    out_qkv = scatter_sum(gw_qkv, grp_size, seq_size)
    out_sums = scatter_sum(sums, grp_size, seq_size)
    return (
        layer_out,
        grad_inputs,
        out_qkv[:, :width],
        out_qkv[:, width : 2 * width],
        out_qkv[:, 2 * width :],
        out_out,
        out_up,
        out_down,
        out_sums[:, 0],
        out_sums[:, 1],
        out_sums[:, 2],
        out_sums[:, 8 : 8 + spread].reshape(-1),
        out_sums[:, 3],
        out_sums[:, 4],
        out_sums[:, 5],
        out_sums[:, 6],
        out_sums[:, 7],
    )


def solution(mesh):
    return jax.shard_map(
        functools.partial(body, mesh.shape["grp"], mesh.shape["seq"]),
        mesh=mesh,
        in_specs=(
            P("grp", None, "seq", None),
            P("grp", None),
            P("grp", None, "seq", None),
            P(("grp", "seq"), None),
            P(("grp", "seq"), None),
            P(("grp", "seq"), None),
            P(("grp", "seq"), None),
            P(("grp", "seq"), None),
            P(("grp", "seq"), None),
            P(("grp", "seq")),
            P(("grp", "seq")),
            P(("grp", "seq")),
            P(("grp", "seq")),
            P(("grp", "seq")),
            P(("grp", "seq")),
            P(("grp", "seq")),
            P(("grp", "seq")),
            P(("grp", "seq")),
        ),
        out_specs=(
            P("grp", None, "seq", None),
            P("grp", None, "seq", None),
            P(("grp", "seq"), None),
            P(("grp", "seq"), None),
            P(("grp", "seq"), None),
            P(("grp", "seq"), None),
            P(("grp", "seq"), None),
            P(("grp", "seq"), None),
            P(("grp", "seq")),
            P(("grp", "seq")),
            P(("grp", "seq")),
            P(("grp", "seq")),
            P(("grp", "seq")),
            P(("grp", "seq")),
            P(("grp", "seq")),
            P(("grp", "seq")),
            P(("grp", "seq")),
        ),
        check_vma=False,
    )
```

```python
import functools

import jax
import jax.numpy as jnp
from jax import lax
from jax.experimental import pallas as pl
from jax.experimental.pallas import tpu as pltpu
from jax.sharding import PartitionSpec as P

HEAD = 64


epsilon = 1e-05
score_scale = 0.125
sqrt_half = 0.7071067811865476
inv_root_tau = 0.3989422804014327


def standardize(token_rows):
    row_mean = jnp.mean(token_rows, -1, keepdims=True)
    centred = token_rows - row_mean
    inverse = lax.rsqrt(jnp.mean(centred * centred, -1, keepdims=True) + epsilon)
    return (centred * inverse, inverse)


def norm_back(grad_out, normed, inverse, gain_vec):
    scaled = grad_out * gain_vec
    grad_rows = inverse * (
        scaled
        - jnp.mean(scaled, -1, keepdims=True)
        - normed * jnp.mean(scaled * normed, -1, keepdims=True)
    )
    return (grad_rows, jnp.sum(grad_out * normed, 0), jnp.sum(grad_out, 0))


def gelu_slope(hidden):
    return (
        0.5 * (1.0 + lax.erf(hidden * sqrt_half))
        + hidden * jnp.exp(-0.5 * hidden * hidden) * inv_root_tau
    )


PAIR = 2 * HEAD
Q_BLOCK = 256
NT = (((1,), (1,)), ((), ()))
f32 = jnp.float32
bf16 = jnp.bfloat16


def head_mask(head, width):
    lane = lax.broadcasted_iota(jnp.int32, (1, width), 1)
    chosen = lane < HEAD if head == 0 else lane >= HEAD
    return chosen.astype(f32).astype(bf16)


def nt(left, right):
    return lax.dot_general(left, right, NT, preferred_element_type=f32)


def attend_kernel(q_ref, ko_ref, kx_ref, vo_ref, vx_ref, bias_ref, out_ref, lse_ref):
    queries = q_ref[...] * jnp.asarray(score_scale, bf16)
    keys = jnp.concatenate([ko_ref[...], kx_ref[...]], 0)
    values_t = jnp.concatenate([vo_ref[...], vx_ref[...]], 0).T
    bias = jnp.concatenate([bias_ref[...]] * 2, 0)
    mixed = []
    for head in range(2):
        scores = nt(keys, queries * head_mask(head, PAIR)) + bias
        row_max = jnp.max(scores, 0, keepdims=True)
        exponent = jnp.exp(scores - row_max)
        row_sum = jnp.sum(exponent, 0, keepdims=True)
        part = jnp.dot(
            values_t[head * HEAD : (head + 1) * HEAD],
            exponent.astype(bf16),
            preferred_element_type=f32,
        )
        mixed.append(part * (1.0 / row_sum))
        lse_ref[0, head : head + 1, :] = row_max + jnp.log(row_sum)
    out_ref[...] = jnp.concatenate(mixed, 0).T.astype(bf16)


def attend_back_kernel(
    q_ref, ko_ref, kx_ref, vo_ref, vx_ref, bias_ref, out_ref, grad_ref, lse_ref,
    dq_ref, dko_ref, dvo_ref, dkx_ref, dvx_ref, dk_acc, dv_acc,
):
    step = pl.program_id(1)
    queries = q_ref[...] * jnp.asarray(score_scale, bf16)
    grads = grad_ref[...]
    keys = jnp.concatenate([ko_ref[...], kx_ref[...]], 0)
    keys_t = keys.T
    values = jnp.concatenate([vo_ref[...], vx_ref[...]], 0)
    bias = jnp.concatenate([bias_ref[...]] * 2, 0)
    inner = (grads.astype(f32) * out_ref[...].astype(f32)).T
    grad_queries = []
    grad_keys = grad_values = None
    for head in range(2):
        mask = head_mask(head, PAIR)
        rows = slice(head * HEAD, (head + 1) * HEAD)
        query_head, grad_head = queries * mask, grads * mask
        scores = nt(keys, query_head) + bias
        weights = jnp.exp(scores - lse_ref[0, head : head + 1, :])
        inner_sum = jnp.sum(inner[rows], 0, keepdims=True)
        grad_scores = (weights * (nt(values, grad_head) - inner_sum)).astype(bf16)
        value_part = jnp.dot(weights.astype(bf16), grad_head, preferred_element_type=f32)
        key_part = jnp.dot(grad_scores, query_head, preferred_element_type=f32)
        grad_values = value_part if head == 0 else grad_values + value_part
        grad_keys = key_part if head == 0 else grad_keys + key_part
        grad_queries.append(jnp.dot(keys_t[rows], grad_scores, preferred_element_type=f32))
    dq_ref[...] = (jnp.concatenate(grad_queries, 0).T * score_scale).astype(bf16)

    @pl.when(step == 0)
    def _():
        dk_acc[...] = grad_keys
        dv_acc[...] = grad_values

    @pl.when(step > 0)
    def _():
        dk_acc[...] += grad_keys
        dv_acc[...] += grad_values

    @pl.when(step == pl.num_programs(1) - 1)
    def _():
        half = dko_ref.shape[0]
        dko_ref[...] = dk_acc[:half].astype(bf16)
        dkx_ref[...] = dk_acc[half:].astype(bf16)
        dvo_ref[...] = dv_acc[:half].astype(bf16)
        dvx_ref[...] = dv_acc[half:].astype(bf16)


def attention_specs(rows, pairs, first):
    whole = lambda shift: pl.BlockSpec((rows, PAIR), lambda p, i: (0, p + first + shift))
    return [
        pl.BlockSpec((Q_BLOCK, PAIR), lambda p, i: (i, p + first)),
        whole(pairs),
        whole(0),
        whole(2 * pairs),
        whole(pairs),
        pl.BlockSpec((rows, Q_BLOCK), lambda p, i: (0, 0)),
    ]


def attend(qkv, kv_other, bias):
    rows, width = qkv.shape[0], qkv.shape[1] // 3
    pairs = width // PAIR
    return pl.pallas_call(
        attend_kernel,
        grid=(pairs, rows // Q_BLOCK),
        in_specs=attention_specs(rows, pairs, 0),
        out_specs=[
            pl.BlockSpec((Q_BLOCK, PAIR), lambda p, i: (i, p)),
            pl.BlockSpec((1, 8, Q_BLOCK), lambda p, i: (p, 0, i)),
        ],
        out_shape=[
            jax.ShapeDtypeStruct((rows, width), bf16),
            jax.ShapeDtypeStruct((pairs, 8, rows), f32),
        ],
        compiler_params=pltpu.CompilerParams(vmem_limit_bytes=40 * 2**20),
        cost_estimate=pl.CostEstimate(
            flops=32 * rows * rows * width,
            bytes_accessed=14 * rows * width,
            transcendentals=2 * rows * rows * width // HEAD,
        ),
    )(qkv, qkv, kv_other, qkv, kv_other, bias)


def attend_back(qkv, kv_other, bias, mixed, grads, lse, first, count):
    rows, width = mixed.shape
    pairs = width // PAIR
    block = lambda: pl.BlockSpec((Q_BLOCK, PAIR), lambda p, i: (i, p + first))
    return pl.pallas_call(
        attend_back_kernel,
        grid=(count, rows // Q_BLOCK),
        in_specs=attention_specs(rows, pairs, first)
        + [block(), block(), pl.BlockSpec((1, 8, Q_BLOCK), lambda p, i: (p + first, 0, i))],
        out_specs=[pl.BlockSpec((Q_BLOCK, PAIR), lambda p, i: (i, p))]
        + [pl.BlockSpec((rows, PAIR), lambda p, i: (0, p))] * 4,
        out_shape=[jax.ShapeDtypeStruct((rows, count * PAIR), bf16)] * 5,
        scratch_shapes=[pltpu.VMEM((2 * rows, PAIR), f32)] * 2,
        compiler_params=pltpu.CompilerParams(vmem_limit_bytes=40 * 2**20),
        cost_estimate=pl.CostEstimate(
            flops=80 * rows * rows * count * PAIR,
            bytes_accessed=24 * rows * count * PAIR,
            transcendentals=4 * rows * rows * count,
        ),
    )(qkv, qkv, kv_other, qkv, kv_other, bias, mixed, grads, lse)


def pick(block, index, axis):
    return lax.dynamic_index_in_dim(block, index, axis, keepdims=False)


def scatter_sum(total, grp_size, seq_size):
    grp, seq = lax.axis_index("grp"), lax.axis_index("seq")
    unit, columns = total.shape[0] // grp_size, total.shape[1]
    left, bit = grp_size, 1
    while left > 1:
        left //= 2
        total = total.reshape(left, 2, unit, columns)
        mine = (grp // bit) % 2
        arrived = lax.ppermute(
            pick(total, 1 - mine, 1).astype(bf16), "grp", [(i, i ^ bit) for i in range(grp_size)]
        )
        total = pick(total, mine, 1) + arrived.astype(f32)
        bit *= 2
    total = total.reshape(seq_size, unit // seq_size, columns)
    result = pick(total, seq, 0)
    for offset in range(1, seq_size):
        arrived = lax.ppermute(
            pick(total, (seq + offset) % seq_size, 0).astype(bf16),
            "seq",
            [(i, (i + offset) % seq_size) for i in range(seq_size)],
        )
        result = result + arrived.astype(f32)
    return result


def body(
    grp_size, seq_size,
    inputs, clip_frames, cotangent,
    w_query, w_key, w_value, w_out, w_up, w_down,
    b_query, b_value, b_out, b_up, b_down,
    gain_one, shift_one, gain_two, shift_two,
):
    axes = ("grp", "seq")
    slot_count, slice_len, width = inputs.shape[1:]
    hidden_width = w_up.shape[1]
    depth = w_query.shape[0]
    spread = hidden_width // width
    row_count = slot_count * slice_len
    grp, seq = lax.axis_index("grp"), lax.axis_index("seq")

    def route(flip):
        moves = []
        for g in range(grp_size):
            for s in range(seq_size):
                slot = (s + flip) % 2
                target = (g // 2 * 2 + s // 2) * seq_size + g % 2 * 2 + slot
                moves.append((g * seq_size + s, target))
        return moves

    routes = (route(0), route(1))
    back_routes = tuple([(b, a) for a, b in moves] for moves in routes)
    swap = [(g, g ^ 1) for g in range(grp_size)]
    parity = seq % 2

    def to_clip(block):
        return jnp.concatenate(
            [
                lax.ppermute(pick(block[0], (parity + flip) % 2, 0), axes, routes[flip])
                for flip in range(2)
            ],
            0,
        )

    def from_clip(rows):
        same, other = (
            lax.ppermute(rows[flip * slice_len : (flip + 1) * slice_len], axes, back_routes[flip])
            for flip in range(2)
        )
        even = parity == 0
        return jnp.stack([jnp.where(even, same, other), jnp.where(even, other, same)])[None]

    vectors = jnp.stack(
        [b_query, b_value, b_out, b_down, gain_one, shift_one, gain_two, shift_two], 1
    )
    vectors = jnp.concatenate([vectors, b_up.reshape(depth, spread)], 1)
    vectors = jnp.pad(vectors, ((0, 0), (0, 128 - vectors.shape[1])))
    early = lax.all_gather(
        jnp.concatenate([w_query, w_key, w_value, vectors], 1), axes, axis=0, tiled=True
    )
    late_shard = jnp.concatenate([w_out, w_up, w_down.reshape(depth, hidden_width)], 1)
    early, late_shard = lax.optimization_barrier((early, late_shard))
    late = lax.all_gather(late_shard, axes, axis=0, tiled=True)
    w_qkv = early[:, : 3 * width]
    columns = early[:, 3 * width :].astype(f32).T
    bq, bv, bo, bd, gain_first, shift_first, gain_second, shift_second = (
        columns[i] for i in range(8)
    )
    bu = columns[8 : 8 + spread].T.reshape(hidden_width)
    wo_full = late[:, :width]
    up_full = late[:, width : width + hidden_width]
    down_full = late[:, width + hidden_width :].reshape(hidden_width, width)

    frames_other = lax.ppermute(clip_frames, "grp", swap)
    frames = jnp.where(seq // 2 == grp % 2, clip_frames, frames_other)[0]
    frame_count = jnp.where(parity == 0, frames[0], frames[1])
    offsets = jnp.arange(row_count, dtype=jnp.int32) % slice_len
    bias = jnp.broadcast_to(
        jnp.where(offsets < frame_count, 0.0, -1e30).astype(f32)[:, None], (row_count, Q_BLOCK)
    )

    token_rows = to_clip(inputs).astype(f32)
    normed_one, inverse_one = standardize(token_rows)
    first_in = (normed_one * gain_first + shift_first).astype(bf16)
    b_qkv = jnp.concatenate([bq, jnp.zeros_like(bq), bv])
    qkv = (jnp.dot(first_in, w_qkv, preferred_element_type=f32) + b_qkv).astype(bf16)
    kv_other = lax.ppermute(qkv[:, width:], "grp", swap)
    kv_other, cotangent = lax.optimization_barrier((kv_other, cotangent))
    parts = [
        lax.ppermute(pick(cotangent[0], (parity + flip) % 2, 0), axes, routes[flip])
        for flip in range(2)
    ]
    mixed_low, lse = attend(qkv, kv_other, bias)
    mixed_low, *parts = lax.optimization_barrier((mixed_low, *parts))
    grad_top = jnp.concatenate(parts, 0)
    middle = token_rows + jnp.dot(mixed_low, wo_full, preferred_element_type=f32) + bo
    normed_two, inverse_two = standardize(middle)
    second_in = (normed_two * gain_second + shift_second).astype(bf16)
    hidden = jnp.dot(second_in, up_full, preferred_element_type=f32) + bu
    active_low = jax.nn.gelu(hidden, approximate=False).astype(bf16)
    result = middle + jnp.dot(active_low, down_full, preferred_element_type=f32) + bd
    layer_out = from_clip(result.astype(bf16))

    grad_rows = grad_top.astype(f32)
    grad_down = jnp.dot(active_low.T, grad_top, preferred_element_type=f32)
    gbias_down = jnp.sum(grad_rows, 0)
    grad_active = jnp.dot(grad_top, down_full.T, preferred_element_type=f32)
    grad_hidden = (grad_active * gelu_slope(hidden)).astype(bf16)
    grad_up = jnp.dot(second_in.T, grad_hidden, preferred_element_type=f32)
    gbias_up = jnp.sum(grad_hidden.astype(f32), 0)
    grad_second = jnp.dot(grad_hidden, up_full.T, preferred_element_type=f32)
    grad_norm_two, grad_gain_two, grad_shift_two = norm_back(
        grad_second, normed_two, inverse_two, gain_second
    )
    grad_middle = grad_rows + grad_norm_two
    grad_branch = grad_middle.astype(bf16)
    grad_out = jnp.dot(mixed_low.T, grad_branch, preferred_element_type=f32)
    gbias_out = jnp.sum(grad_branch.astype(f32), 0)
    grad_mixed = jnp.dot(grad_branch, wo_full.T, preferred_element_type=f32).astype(bf16)

    out_down = scatter_sum(grad_down, grp_size, seq_size)
    out_up = scatter_sum(grad_up, grp_size, seq_size)
    out_out = scatter_sum(grad_out, grp_size, seq_size)

    pairs = width // PAIR
    count = 1
    grad_q, grad_k, grad_v = [], [], []
    for start in range(0, pairs, count):
        dq, dko, dvo, dkx, dvx = attend_back(
            qkv, kv_other, bias, mixed_low, grad_mixed, lse, start, count
        )
        grad_q.append(dq)
        for own, other, kept in ((dko, dkx, grad_k), (dvo, dvx, grad_v)):
            arrived = lax.ppermute(other, "grp", swap)
            kept.append((own.astype(f32) + arrived.astype(f32)).astype(bf16))
    grad_qkv = jnp.concatenate(grad_q + grad_k + grad_v, 1)
    gw_qkv = jnp.dot(first_in.T, grad_qkv, preferred_element_type=f32)
    gbias_qkv = jnp.sum(grad_qkv.astype(f32), 0)
    grad_first = lax.dot_general(grad_qkv, w_qkv, NT, preferred_element_type=f32)
    grad_norm_one, grad_gain_one, grad_shift_one = norm_back(
        grad_first, normed_one, inverse_one, gain_first
    )
    grad_inputs = from_clip((grad_middle + grad_norm_one).astype(bf16))
    sums = jnp.stack(
        [
            gbias_qkv[:width], gbias_qkv[2 * width :], gbias_out, gbias_down,
            grad_gain_one, grad_shift_one, grad_gain_two, grad_shift_two,
        ]
    )
    sums = jnp.concatenate([sums, gbias_up.reshape(width, spread).T], 0)
    sums = jnp.pad(sums, ((0, 128 - sums.shape[0]), (0, 0))).T
    out_qkv = scatter_sum(gw_qkv, grp_size, seq_size)
    out_sums = scatter_sum(sums, grp_size, seq_size)
    return (
        layer_out,
        grad_inputs,
        out_qkv[:, :width],
        out_qkv[:, width : 2 * width],
        out_qkv[:, 2 * width :],
        out_out,
        out_up,
        out_down,
        out_sums[:, 0],
        out_sums[:, 1],
        out_sums[:, 2],
        out_sums[:, 8 : 8 + spread].reshape(-1),
        out_sums[:, 3],
        out_sums[:, 4],
        out_sums[:, 5],
        out_sums[:, 6],
        out_sums[:, 7],
    )


def solution(mesh):
    return jax.shard_map(
        functools.partial(body, mesh.shape["grp"], mesh.shape["seq"]),
        mesh=mesh,
        in_specs=(
            P("grp", None, "seq", None),
            P("grp", None),
            P("grp", None, "seq", None),
            P(("grp", "seq"), None),
            P(("grp", "seq"), None),
            P(("grp", "seq"), None),
            P(("grp", "seq"), None),
            P(("grp", "seq"), None),
            P(("grp", "seq"), None),
            P(("grp", "seq")),
            P(("grp", "seq")),
            P(("grp", "seq")),
            P(("grp", "seq")),
            P(("grp", "seq")),
            P(("grp", "seq")),
            P(("grp", "seq")),
            P(("grp", "seq")),
            P(("grp", "seq")),
        ),
        out_specs=(
            P("grp", None, "seq", None),
            P("grp", None, "seq", None),
            P(("grp", "seq"), None),
            P(("grp", "seq"), None),
            P(("grp", "seq"), None),
            P(("grp", "seq"), None),
            P(("grp", "seq"), None),
            P(("grp", "seq"), None),
            P(("grp", "seq")),
            P(("grp", "seq")),
            P(("grp", "seq")),
            P(("grp", "seq")),
            P(("grp", "seq")),
            P(("grp", "seq")),
            P(("grp", "seq")),
            P(("grp", "seq")),
            P(("grp", "seq")),
        ),
        check_vma=False,
    )
```
